32 devices in a mesh: gx: 8 (over y, x, core), gy: 4 (over z).
Axes of the slice: x: 2, y: 2, z: 4, core: 2. Of those that a mesh axis runs over, the one named last changes fastest.
Arguments:
- volumes: bfloat16 [2, 64, 256, 1024], P(None, None, 'gy', 'gx'), may hold values from -6 to 6
- peaks: int32 [3, 8, 32], P(None, 'gy', 'gx'), may hold values from -8 to 8
- valid: int32 [8, 32], P('gy', 'gx'), may hold values 0 or 1
Outputs:
- displacement: float32 [3, 8, 32], P(None, 'gy', 'gx')
- peak_score: float32 [8, 32], P('gy', 'gx')
The draws below stay inside these ranges and needn't reach their ends.
All inputs are finite; a program needn't handle non-finite values. No bound on the sum of `valid` on one device may be relied on, other than what follows from the above.
Results may differ from the reference program's by a relative error of at most 0.0089.
Values may be sent and summed in bfloat16 or wider, within the bound.
A program may use at most 64 MiB of HBM per device.

```python
import math
import jax
import jax.numpy as jnp
from jax import lax

B = 64
SWEEPS = 3
PEAK = 8
NGX = 32
NGY = 8
NX = 1024
NY = 256


def with_ends(array, rng, low, largest):
    longest = array.shape.index(max(array.shape))
    spots = []
    for shift in (0, 1):
        where = [jax.random.randint(jax.random.fold_in(rng, axis), (), 0, length) for axis, length in enumerate(array.shape)]
        where[longest] = (where[longest] + shift) % array.shape[longest]
        spots.append(tuple(where))
    return array.at[spots[0]].set(low).at[spots[1]].set(largest)


def level_of(own_key, dims, shards, low, top_value):
    loudness, own = 1.0, jax.random.fold_in(own_key, 6)
    for position, shards_of in shards:
        draws = jnp.exp(jax.random.uniform(jax.random.fold_in(own, position), (shards_of,), jnp.float32, low / len(shards), top_value / len(shards)))
        loudness = loudness * jnp.repeat(draws, dims[position] // shards_of).reshape([-1 if axis == position else 1 for axis in range(len(dims))])
    return loudness


def gaussian(own_key, extent, spread, reach, pieces=(), held_as=jnp.bfloat16):
    array = spread * jax.random.normal(own_key, extent, jnp.float32)
    if pieces:
        array = array * level_of(own_key, extent, pieces, -0.22, 0.18)
    return jnp.clip(array, -reach, reach).astype(held_as)


def setup_inputs(seed: int = 0) -> dict:
    streams_of = jax.random.split(jax.random.key(seed), 4)
    volumes = gaussian(streams_of[0], (2, B, NY, NX), 1.0, 6.0, ((2, 4), (3, 8)))
    peaks = with_ends(jax.random.randint(streams_of[1], (3, NGY, NGX), 0 - PEAK, PEAK + 1), jax.random.fold_in(streams_of[1], 1), 0 - PEAK, PEAK).astype(jnp.int32)
    valid = with_ends((jax.random.randint(streams_of[2], (NGY, NGX), 0, 4) < 3).astype(jnp.int32), jax.random.fold_in(streams_of[2], 1), 0, 1)
    return {"volumes": volumes, "peaks": peaks, "valid": valid}


def dft_tables(length):
    counter = jnp.arange(length, dtype=jnp.int32)
    product = counter[:, None] * counter[None, :] % length
    angle = product.astype(jnp.float32) * (2.0 * math.pi / length)
    factor = 1.0 / math.sqrt(length)
    return ((jnp.cos(angle) * factor).astype(jnp.bfloat16), (jnp.sin(angle) * factor).astype(jnp.bfloat16))

def contract(form, left, table):
    return jnp.einsum(form, left.astype(jnp.float32), table.astype(jnp.float32))

def spectra(pair, cosine, sine):
    real_one = contract('vzyx,xk->vzyk', pair, cosine).astype(jnp.bfloat16)
    imag_one = (-contract('vzyx,xk->vzyk', pair, sine)).astype(jnp.bfloat16)
    real_two = (contract('vzyx,yk->vzkx', real_one, cosine) + contract('vzyx,yk->vzkx', imag_one, sine)).astype(jnp.bfloat16)
    imag_two = (contract('vzyx,yk->vzkx', imag_one, cosine) - contract('vzyx,yk->vzkx', real_one, sine)).astype(jnp.bfloat16)
    real_three = contract('vzyx,zk->vkyx', real_two, cosine) + contract('vzyx,zk->vkyx', imag_two, sine)
    imag_three = contract('vzyx,zk->vkyx', imag_two, cosine) - contract('vzyx,zk->vkyx', real_two, sine)
    return (real_three, imag_three)

def phases(offset, length):
    counter = jnp.arange(length, dtype=jnp.int32)
    shifts = offset + jnp.arange(3, dtype=jnp.int32) - 1
    product = jnp.mod(shifts[:, None] * counter[None, :], length)
    angle = product.astype(jnp.float32) * (2.0 * math.pi / length)
    return (jnp.cos(angle).astype(jnp.bfloat16), jnp.sin(angle).astype(jnp.bfloat16))

def evaluate(real_r, imag_r, peak, length):
    highest = lax.Precision.HIGHEST
    cos_x, sin_x = phases(peak[0], length)
    cos_y, sin_y = phases(peak[1], length)
    cos_z, sin_z = phases(peak[2], length)
    real_w = real_r.astype(jnp.float32)
    imag_w = imag_r.astype(jnp.float32)
    cos_x = cos_x.astype(jnp.float32)
    sin_x = sin_x.astype(jnp.float32)
    cos_y = cos_y.astype(jnp.float32)
    sin_y = sin_y.astype(jnp.float32)
    cos_z = cos_z.astype(jnp.float32)
    sin_z = sin_z.astype(jnp.float32)
    along_re = jnp.einsum('zyx,ax->zya', real_w, cos_x) - jnp.einsum('zyx,ax->zya', imag_w, sin_x)
    along_im = jnp.einsum('zyx,ax->zya', real_w, sin_x) + jnp.einsum('zyx,ax->zya', imag_w, cos_x)
    second_re = jnp.einsum('zya,by->zba', along_re, cos_y, precision=highest) - jnp.einsum('zya,by->zba', along_im, sin_y, precision=highest)
    second_im = jnp.einsum('zya,by->zba', along_re, sin_y, precision=highest) + jnp.einsum('zya,by->zba', along_im, cos_y, precision=highest)
    cube = jnp.einsum('zba,cz->cba', second_re, cos_z, precision=highest) - jnp.einsum('zba,cz->cba', second_im, sin_z, precision=highest)
    return cube * (1.0 / (length * math.sqrt(length)))

def block_result(pair, peak, cosine, sine, length):
    real_f, imag_f = spectra(pair, cosine, sine)
    magnitude = jnp.sqrt(real_f[0] * real_f[0] + imag_f[0] * imag_f[0]) * jnp.sqrt(real_f[1] * real_f[1] + imag_f[1] * imag_f[1]) + 1.0
    real_r = ((real_f[0] * real_f[1] + imag_f[0] * imag_f[1]) / magnitude).astype(jnp.bfloat16)
    imag_r = ((imag_f[0] * real_f[1] - real_f[0] * imag_f[1]) / magnitude).astype(jnp.bfloat16)
    cube = evaluate(real_r, imag_r, peak, length)
    centre = cube[1, 1, 1]
    lower = jnp.stack([cube[1, 1, 0], cube[1, 0, 1], cube[0, 1, 1]])
    upper = jnp.stack([cube[1, 1, 2], cube[1, 2, 1], cube[2, 1, 1]])
    shift = jnp.tanh((lower - upper) / (jnp.abs(lower + upper - 2.0 * centre) + 0.5))
    return (centre, peak.astype(jnp.float32) + shift)

def relax(padded, data, mask, spacing):
    east = padded[:, 1:-1, 2:]
    west = padded[:, 1:-1, :-2]
    north = padded[:, 2:, 1:-1]
    south = padded[:, :-2, 1:-1]
    north_east = padded[:, 2:, 2:]
    north_west = padded[:, 2:, :-2]
    south_east = padded[:, :-2, 2:]
    south_west = padded[:, :-2, :-2]
    x_xi = spacing + 0.5 * (east[0] - west[0])
    y_xi = 0.5 * (east[1] - west[1])
    x_eta = 0.5 * (north[0] - south[0])
    y_eta = spacing + 0.5 * (north[1] - south[1])
    alpha = x_eta * x_eta + y_eta * y_eta
    beta = x_xi * x_eta + y_xi * y_eta
    gamma = x_xi * x_xi + y_xi * y_xi
    smooth = (alpha * (east + west) + gamma * (north + south) - 0.5 * beta * (north_east - north_west - south_east + south_west)) / (2.0 * (alpha + gamma))
    return smooth + 0.5 * mask * (data - smooth)

def reference(volumes, peaks, valid):
    length = volumes.shape[1]
    margin = length // 4
    stride = length // 2
    grid_y = peaks.shape[1]
    grid_x = peaks.shape[2]
    padded = jnp.pad(volumes, ((0, 0), (0, 0), (margin, margin), (margin, margin)))
    cosine, sine = dft_tables(length)
    flat_peaks = peaks.reshape(3, grid_y * grid_x).T
    zero = jnp.zeros((), jnp.int32)

    def one_block(index):
        row_index = (index // grid_x).astype(jnp.int32)
        col_index = (index % grid_x).astype(jnp.int32)
        pair = lax.dynamic_slice(padded, (zero, zero, row_index * stride, col_index * stride), (2, length, length, length))
        return block_result(pair, flat_peaks[index], cosine, sine, length)
    scores, data = lax.map(one_block, jnp.arange(grid_y * grid_x, dtype=jnp.int32))
    peak_score = scores.reshape(grid_y, grid_x)
    data = data.T.reshape(3, grid_y, grid_x)
    mask = valid.astype(jnp.float32)
    moved = mask * data
    for sweep_index in range(SWEEPS):
        moved = relax(jnp.pad(moved, ((0, 0), (1, 1), (1, 1))), data, mask, float(stride))
    return (moved, peak_score)
```

```python
import functools
import math

import jax
import jax.numpy as jnp
import ml_dtypes
import numpy as np
from jax import lax
from jax.experimental import pallas as pl
from jax.experimental.pallas import tpu as pltpu
from jax.sharding import PartitionSpec as P

SWEEPS = 3
ZSTEP = 4


def padded_2(array, sides, width):
    for axis, dim in sides:
        devices, length = (lax.axis_size(axis), array.shape[dim])
        up = [(i, (i + 1) % devices) for i in range(devices - 1)]
        down = [(j, i) for i, j in up]
        last = lax.slice_in_dim(array, length - width, length, axis=dim)
        initial = lax.slice_in_dim(array, 0, width, axis=dim)
        before = lax.ppermute(last, axis, up)
        after = lax.ppermute(initial, axis, down)
        array = jnp.concatenate([before, array, after], axis=dim)
    return array


def tables(length, grid_x, grid_y):
    counter = np.arange(length)
    angle = (counter[:, None] * counter[None, :] % length).astype(np.float32) * np.float32(
        2.0 * math.pi / length
    )
    factor = np.float32(1.0 / math.sqrt(length))
    cosine = (np.cos(angle) * factor).astype(ml_dtypes.bfloat16)
    sine = (np.sin(angle) * factor).astype(ml_dtypes.bfloat16)
    stride = length // 2
    half = length // 2 + 1
    width = stride * grid_x + stride
    height = stride * grid_y + stride
    along_x = np.zeros((width, 2, grid_x, length), ml_dtypes.bfloat16)
    for i in range(grid_x):
        along_x[i * stride : i * stride + length, 0, i] = cosine
        along_x[i * stride : i * stride + length, 1, i] = -sine
    lines = grid_y * half
    padded = -(-lines // 8) * 8
    along_y = np.zeros((2, padded, 2, height), ml_dtypes.bfloat16)
    for j in range(grid_y):
        rows = slice(j * half, (j + 1) * half)
        window = slice(j * stride, j * stride + length)
        along_y[0, rows, 0, window] = cosine[:half]
        along_y[0, rows, 1, window] = sine[:half]
        along_y[1, rows, 0, window] = -sine[:half]
        along_y[1, rows, 1, window] = cosine[:half]
    along_z = np.block([[cosine, sine], [-sine, cosine]])
    return (
        along_x.reshape(width, 2 * grid_x * length),
        along_y.reshape(2 * padded, 2 * height),
        along_z,
    )


def spectrum_kernel(
    grid_x, grid_y, vol, table_x, table_y, table_z, table_e, cos_y, sin_y, out, first, second
):
    length = vol.shape[1]
    height = vol.shape[2]
    half = length // 2 + 1
    lanes = grid_x * length
    padded = table_y.shape[0] // 2
    pieces = 2 * lanes // 128

    def slab(step, carry):
        z0 = step * ZSTEP
        for v in range(2):
            rows = vol[v, pl.ds(z0, ZSTEP)].reshape(ZSTEP * height, vol.shape[3])
            one = jnp.dot(rows, table_x[...], preferred_element_type=jnp.float32)
            first[v] = one.astype(jnp.bfloat16)
        for i in range(ZSTEP):
            ys = slice(i * height, (i + 1) * height)
            right = jnp.concatenate(
                [
                    jnp.concatenate([first[0, ys, :lanes], first[1, ys, :lanes]], axis=1),
                    jnp.concatenate([first[0, ys, lanes:], first[1, ys, lanes:]], axis=1),
                ],
                axis=0,
            )
            two = jnp.dot(table_y[...], right, preferred_element_type=jnp.float32)
            for c in range(2):
                for t in range(pieces):
                    second[t, pl.ds(c * length + z0 + i, padded, stride=2 * length), :] = two[
                        c * padded : (c + 1) * padded, t * 128 : (t + 1) * 128
                    ]
        return carry

    lax.fori_loop(0, length // ZSTEP, slab, 0)

    group = lax.broadcasted_iota(jnp.int32, (8, lanes), 1) // length

    for j in range(grid_y):

        def line(ky, sums):
            base = pl.multiple_of((j * half + ky) * 2 * length, 2 * length)
            right = jnp.concatenate(
                [second[t, pl.ds(base, 2 * length), :].astype(jnp.bfloat16) for t in range(pieces)],
                axis=1,
            )
            three = jnp.dot(table_z[...], right, preferred_element_type=jnp.float32)
            re1, im1 = three[:length, :lanes], three[length:, :lanes]
            re2, im2 = three[:length, lanes:], three[length:, lanes:]
            size = (re1 * re1 + im1 * im1) * (re2 * re2 + im2 * im2)
            scale = 1.0 / (jnp.sqrt(size) + 1.0)
            real_r = ((re1 * re2 + im1 * im2) * scale).astype(jnp.bfloat16)
            imag_r = ((im1 * re2 - re1 * im2) * scale).astype(jnp.bfloat16)
            both = jnp.concatenate([real_r, imag_r], axis=0)
            along = jnp.dot(table_e[j], both, preferred_element_type=jnp.float32)
            own = along[:8]
            for i in range(1, grid_x):
                own = jnp.where(group == i, along[8 * i : 8 * i + 8], own)
            new = []
            for o in range(3):
                new.append(sums[2 * o] + own * cos_y[j, o, pl.ds(ky, 1), :])
                new.append(sums[2 * o + 1] + own * sin_y[j, o, pl.ds(ky, 1), :])
            return tuple(new)

        zero = jnp.zeros((8, lanes), jnp.float32)
        sums = lax.fori_loop(0, half, line, (zero,) * 6)
        for n in range(6):
            out[j, n] = sums[n]


def phases(offset, length):
    counter = jnp.arange(length, dtype=jnp.int32)
    shifts = offset[..., None] + jnp.arange(3, dtype=jnp.int32) - 1
    product = jnp.mod(shifts[..., None] * counter, length)
    angle = product.astype(jnp.float32) * (2.0 * math.pi / length)
    return (jnp.cos(angle).astype(jnp.bfloat16), jnp.sin(angle).astype(jnp.bfloat16))


def relax(padded, data, mask, spacing):
    east = padded[:, 1:-1, 2:]
    west = padded[:, 1:-1, :-2]
    north = padded[:, 2:, 1:-1]
    south = padded[:, :-2, 1:-1]
    north_east = padded[:, 2:, 2:]
    north_west = padded[:, 2:, :-2]
    south_east = padded[:, :-2, 2:]
    south_west = padded[:, :-2, :-2]
    x_xi = spacing + 0.5 * (east[0] - west[0])
    y_xi = 0.5 * (east[1] - west[1])
    x_eta = 0.5 * (north[0] - south[0])
    y_eta = spacing + 0.5 * (north[1] - south[1])
    alpha = x_eta * x_eta + y_eta * y_eta
    beta = x_xi * x_eta + y_xi * y_eta
    gamma = x_xi * x_xi + y_xi * y_xi
    smooth = (
        alpha * (east + west)
        + gamma * (north + south)
        - 0.5 * beta * (north_east - north_west - south_east + south_west)
    ) / (2.0 * (alpha + gamma))
    return smooth + 0.5 * mask * (data - smooth)


def body(volumes, peaks, valid):
    length = volumes.shape[1]
    margin = length // 4
    stride = length // 2
    half = length // 2 + 1
    _, grid_y, grid_x = peaks.shape
    lanes = grid_x * length
    padded = padded_2(volumes, (("gx", 3), ("gy", 2)), margin)
    table_x, table_y, table_z = tables(length, grid_x, grid_y)
    cosine, sine = phases(peaks, length)
    cos_z, sin_z = cosine[2], sine[2]
    rows_re = jnp.concatenate([cos_z, -sin_z], axis=-1)
    rows_im = jnp.concatenate([sin_z, cos_z], axis=-1)
    table_e = jnp.stack([rows_re, rows_im], axis=3).reshape(grid_y, grid_x, 6, 2 * length)
    table_e = jnp.pad(table_e, ((0, 0), (0, 0), (0, 2), (0, 0))).reshape(
        grid_y, grid_x * 8, 2 * length
    )
    weight = np.full((half,), 2.0, np.float32)
    weight[0] = weight[-1] = 1.0

    def spread(table):
        table = table[..., :half].astype(jnp.float32) * weight
        table = jnp.broadcast_to(
            table.transpose(0, 2, 3, 1)[..., None], (grid_y, 3, half, grid_x, length)
        )
        return table.reshape(grid_y, 3, half, lanes)

    sums = pl.pallas_call(
        functools.partial(spectrum_kernel, grid_x, grid_y),
        out_shape=jax.ShapeDtypeStruct((grid_y, 6, 8, lanes), jnp.float32),
        in_specs=[pl.BlockSpec(memory_space=pltpu.VMEM)] * 7,
        out_specs=pl.BlockSpec(memory_space=pltpu.VMEM),
        scratch_shapes=[
            pltpu.VMEM((2, ZSTEP * padded.shape[2], 2 * lanes), jnp.bfloat16),
            pltpu.VMEM((2 * lanes // 128, table_y.shape[0] * length, 128), jnp.float32),
        ],
        compiler_params=pltpu.CompilerParams(vmem_limit_bytes=56 * 1024 * 1024),
        name="spectrum",
    )(padded, table_x, table_y, table_z, table_e, spread(cosine[1]), spread(sine[1]))

    sums = sums.reshape(grid_y, 3, 2, 8, grid_x, length)
    factor = 1.0 / (length * math.sqrt(length))
    cos_x = cosine[0].astype(jnp.float32) * factor
    sin_x = sine[0].astype(jnp.float32) * factor

    def corr(ox, oy, oz):
        real = sums[:, oy, 0, 2 * oz] - sums[:, oy, 1, 2 * oz + 1]
        imag = sums[:, oy, 1, 2 * oz] + sums[:, oy, 0, 2 * oz + 1]
        return jnp.sum(real * cos_x[:, :, ox] - imag * sin_x[:, :, ox], axis=-1)

    centre = corr(1, 1, 1)
    lower = jnp.stack([corr(0, 1, 1), corr(1, 0, 1), corr(1, 1, 0)])
    upper = jnp.stack([corr(2, 1, 1), corr(1, 2, 1), corr(1, 1, 2)])
    shift = jnp.tanh((lower - upper) / (jnp.abs(lower + upper - 2.0 * centre) + 0.5))
    data = peaks.astype(jnp.float32) + shift
    mask = valid.astype(jnp.float32)
    moved = mask * data
    for _ in range(SWEEPS):
        rimmed = padded_2(moved, (("gx", 2), ("gy", 1)), 1)
        moved = relax(rimmed, data, mask, float(stride))
    return (moved, centre)


def solution(mesh):
    return jax.shard_map(
        body,
        mesh=mesh,
        in_specs=(P(None, None, "gy", "gx"), P(None, "gy", "gx"), P("gy", "gx")),
        out_specs=(P(None, "gy", "gx"), P("gy", "gx")),
        check_vma=False,
    )
```

```python
import functools
import math

import jax
import jax.numpy as jnp
import ml_dtypes
import numpy as np
from jax import lax
from jax.experimental import pallas as pl
from jax.experimental.pallas import tpu as pltpu
from jax.sharding import PartitionSpec as P

SWEEPS = 3
ZSTEP = 4


PARTS = 4
GROUP = 8
PITCH = 136
SIDES = [(dx, dy) for dy in (-1, 0, 1) for dx in (-1, 0, 1) if (dx, dy) != (0, 0)]


def tables(length, grid_x, grid_y):
    counter = np.arange(length)
    angle = (counter[:, None] * counter[None, :] % length).astype(np.float32) * np.float32(
        2.0 * math.pi / length
    )
    factor = np.float32(1.0 / math.sqrt(length))
    cosine = (np.cos(angle) * factor).astype(ml_dtypes.bfloat16)
    sine = (np.sin(angle) * factor).astype(ml_dtypes.bfloat16)
    stride = length // 2
    half = length // 2 + 1
    width = stride * grid_x + stride
    height = stride * grid_y + stride
    along_x = np.zeros((width, 2, grid_x, length), ml_dtypes.bfloat16)
    for i in range(grid_x):
        along_x[i * stride : i * stride + length, 0, i] = cosine
        along_x[i * stride : i * stride + length, 1, i] = -sine
    lines = grid_y * half
    padded = -(-lines // 8) * 8
    along_y = np.zeros((2, padded, 2, height), ml_dtypes.bfloat16)
    for j in range(grid_y):
        rows = slice(j * half, (j + 1) * half)
        window = slice(j * stride, j * stride + length)
        along_y[0, rows, 0, window] = cosine[:half]
        along_y[0, rows, 1, window] = sine[:half]
        along_y[1, rows, 0, window] = -sine[:half]
        along_y[1, rows, 1, window] = cosine[:half]
    along_z = np.block([[cosine, sine], [-sine, cosine]])
    margin = stride // 2
    own = width - 2 * margin
    along_x = along_x.reshape(width, 2 * grid_x * length)
    order = np.zeros((2 * own, along_x.shape[1]), ml_dtypes.bfloat16)
    order[:own] = along_x[margin : margin + own]
    order[own : own + margin] = along_x[:margin]
    order[own + margin : own + 2 * margin] = along_x[margin + own :]
    return (
        order,
        along_y.reshape(2 * padded, 2 * height),
        along_z,
    )


def strip_tables(margin, own):
    pack = np.zeros((GROUP, own, 2, GROUP, margin), ml_dtypes.bfloat16)
    unpack = np.zeros((2, GROUP, margin, GROUP, own), ml_dtypes.bfloat16)
    for g in range(GROUP):
        for m in range(margin):
            pack[g, m, 0, g, m] = 1
            pack[g, own - margin + m, 1, g, m] = 1
            unpack[0, g, m, g, m] = 1
            unpack[1, g, m, g, margin + m] = 1
    return (
        pack.reshape(GROUP * own, 2 * GROUP * margin),
        unpack.reshape(2 * GROUP * margin, GROUP * own),
    )


def inside(dx, dy):
    x = lax.axis_index("gx") + dx
    y = lax.axis_index("gy") + dy
    return (x >= 0) & (x < lax.axis_size("gx")) & (y >= 0) & (y < lax.axis_size("gy"))


def greet(sides):
    barrier = pltpu.get_barrier_semaphore()
    for dx, dy in sides:

        @pl.when(inside(dx, dy))
        def _():
            pl.semaphore_signal(
                barrier,
                inc=1,
                device_id={"gx": lax.axis_index("gx") + dx, "gy": lax.axis_index("gy") + dy},
                device_id_type=pl.DeviceIdType.MESH,
            )

    pl.semaphore_wait(barrier, sum(inside(dx, dy).astype(jnp.int32) for dx, dy in sides))


def spectrum_kernel(
    grid_x,
    grid_y,
    vol,
    pack,
    unpack,
    table_x,
    table_y,
    table_z,
    table_e,
    cos_y,
    sin_y,
    out,
    first,
    second,
    strip,
    side_y,
    side_x,
    margins,
    send_sem,
    recv_sem,
):
    length = vol.shape[1]
    tall = vol.shape[2]
    own = vol.shape[3]
    margin = length // 4
    height = tall + 2 * margin
    depth = length // PARTS
    chunks = depth // GROUP

    def copy(dx, dy, part):
        rows = {-1: pl.ds(0, margin), 0: pl.ds(0, tall), 1: pl.ds(tall - margin, margin)}[dy]
        if dx == 0:
            zs = pl.ds(part * depth, depth)
            src = vol.at[:, zs, rows, :]
            dst = side_y.at[(1 - dy) // 2, :, zs, :, :]
        else:
            cs = pl.ds(part * chunks, chunks)
            to = {
                1: pl.ds(0, margin),
                0: pl.ds(margin, tall),
                -1: pl.ds(tall + margin, margin),
            }[dy]
            src = strip.at[(1 + dx) // 2, cs, :, rows, :]
            dst = side_x.at[(1 - dx) // 2, cs, :, to, :]
        n = SIDES.index((dx, dy))
        return pltpu.make_async_remote_copy(
            src_ref=src,
            dst_ref=dst,
            send_sem=send_sem.at[n, part],
            recv_sem=recv_sem.at[n, part],
            device_id={"gx": lax.axis_index("gx") + dx, "gy": lax.axis_index("gy") + dy},
            device_id_type=pl.DeviceIdType.MESH,
        )

    for side, (dx, dy) in enumerate(((0, -1), (0, 1))):

        @pl.when(jnp.logical_not(inside(dx, dy)))
        def _():
            side_y[side] = jnp.zeros(side_y.shape[1:], side_y.dtype)

    for side, dx in enumerate((-1, 1)):
        for dy, lo, count in ((-1, 0, margin), (0, margin, tall), (1, margin + tall, margin)):

            @pl.when(jnp.logical_not(inside(dx, dy)))
            def _():
                side_x[side, :, :, lo : lo + count, :] = jnp.zeros(
                    (side_x.shape[1], 2, count, side_x.shape[4]), side_x.dtype
                )

    greet(SIDES)

    def send_rows(part, carry):
        for dx, dy in SIDES:
            if dx == 0:

                @pl.when(inside(dx, dy))
                def _():
                    copy(dx, dy, part).start()

        return carry

    lax.fori_loop(0, PARTS, send_rows, 0)

    def send_strips(part, carry):
        for i in range(chunks):
            c = part * chunks + i
            wide = jnp.concatenate(
                [vol[:, c * GROUP + g].reshape(2 * tall, own) for g in range(GROUP)], axis=1
            )
            packed = jnp.dot(wide, pack[...], preferred_element_type=jnp.float32)
            packed = packed.astype(jnp.bfloat16).reshape(2, tall, 2 * GROUP * margin)
            strip[0, c] = packed[:, :, : GROUP * margin]
            strip[1, c] = packed[:, :, GROUP * margin :]
        for dx, dy in SIDES:
            if dx != 0:

                @pl.when(inside(dx, dy))
                def _():
                    copy(dx, dy, part).start()

        return carry

    lax.fori_loop(0, PARTS, send_strips, 0)

    half = length // 2 + 1
    lanes = grid_x * length
    padded = table_y.shape[0] // 2
    pieces = 2 * lanes // 128

    def slab(step, carry):
        z0 = step * ZSTEP
        for v in range(2):
            zs = pl.ds(z0, ZSTEP)
            rows = jnp.concatenate([side_y[0, v, zs], vol[v, zs], side_y[1, v, zs]], axis=1)
            rows = jnp.concatenate([rows, margins[v, zs]], axis=2)
            rows = rows.reshape(ZSTEP * height, 2 * own)
            one = jnp.dot(rows, table_x[...], preferred_element_type=jnp.float32)
            first[v] = one.astype(jnp.bfloat16)
        for i in range(ZSTEP):
            ys = slice(i * height, (i + 1) * height)
            right = jnp.concatenate(
                [
                    jnp.concatenate([first[0, ys, :lanes], first[1, ys, :lanes]], axis=1),
                    jnp.concatenate([first[0, ys, lanes:], first[1, ys, lanes:]], axis=1),
                ],
                axis=0,
            )
            two = jnp.dot(table_y[...], right, preferred_element_type=jnp.float32)
            for c in range(2):
                for t in range(pieces):
                    second[t, pl.ds(c * length + z0 + i, padded, stride=PITCH), :] = two[
                        c * padded : (c + 1) * padded, t * 128 : (t + 1) * 128
                    ]
        return carry

    def take(part, carry):
        for dx, dy in SIDES:

            @pl.when(inside(-dx, -dy))
            def _():
                copy(dx, dy, part).wait_recv()

        for i in range(chunks):
            c = part * chunks + i
            wide = jnp.concatenate(
                [side_x[s, c].reshape(2 * height, GROUP * margin) for s in range(2)], axis=1
            )
            apart = jnp.dot(wide, unpack[...], preferred_element_type=jnp.float32)
            apart = apart.astype(jnp.bfloat16).reshape(2, height, GROUP * own)
            for g in range(GROUP):
                margins[:, c * GROUP + g] = apart[:, :, g * own : (g + 1) * own]
        steps = depth // ZSTEP
        return lax.fori_loop(part * steps, (part + 1) * steps, slab, carry)

    lax.fori_loop(0, PARTS, take, 0)

    group = lax.broadcasted_iota(jnp.int32, (8, lanes), 1) // length

    for j in range(grid_y):

        def line(ky, sums):
            base = pl.multiple_of((j * half + ky) * PITCH, 8)
            right = jnp.concatenate(
                [second[t, pl.ds(base, 2 * length), :].astype(jnp.bfloat16) for t in range(pieces)],
                axis=1,
            )
            three = jnp.dot(table_z[...], right, preferred_element_type=jnp.float32)
            re1, im1 = three[:length, :lanes], three[length:, :lanes]
            re2, im2 = three[:length, lanes:], three[length:, lanes:]
            size = (re1 * re1 + im1 * im1) * (re2 * re2 + im2 * im2)
            scale = 1.0 / (jnp.sqrt(size) + 1.0)
            real_r = ((re1 * re2 + im1 * im2) * scale).astype(jnp.bfloat16)
            imag_r = ((im1 * re2 - re1 * im2) * scale).astype(jnp.bfloat16)
            both = jnp.concatenate([real_r, imag_r], axis=0)
            along = jnp.dot(table_e[j], both, preferred_element_type=jnp.float32)
            own = along[:8]
            for i in range(1, grid_x):
                own = jnp.where(group == i, along[8 * i : 8 * i + 8], own)
            new = []
            for o in range(3):
                new.append(sums[2 * o] + own * cos_y[j, o, pl.ds(ky, 1), :])
                new.append(sums[2 * o + 1] + own * sin_y[j, o, pl.ds(ky, 1), :])
            return tuple(new)

        zero = jnp.zeros((8, lanes), jnp.float32)
        sums = lax.fori_loop(0, half, line, (zero,) * 6)
        for n in range(6):
            out[j, n] = sums[n]

    def sent(part, carry):
        for dx, dy in SIDES:

            @pl.when(inside(dx, dy))
            def _():
                copy(dx, dy, part).wait_send()

        return carry

    lax.fori_loop(0, PARTS, sent, 0)


def reach_of(grid_x, grid_y):
    far_x, far_y = -(-SWEEPS // grid_x), -(-SWEEPS // grid_y)
    return far_x, far_y


def partners(grid_x, grid_y):
    far_x, far_y = reach_of(grid_x, grid_y)
    return [
        (dx, dy)
        for dy in range(-far_y, far_y + 1)
        for dx in range(-far_x, far_x + 1)
        if (dx, dy) != (0, 0)
    ]


def sweep_kernel(grid_x, grid_y, spacing, mine, out, inbox, grid, send_sem, recv_sem):
    sides = partners(grid_x, grid_y)
    far_x, far_y = reach_of(grid_x, grid_y)
    tall, wide = grid.shape[1:]

    def copy(n):
        dx, dy = sides[n]
        return pltpu.make_async_remote_copy(
            src_ref=mine,
            dst_ref=inbox.at[n],
            send_sem=send_sem.at[n],
            recv_sem=recv_sem.at[n],
            device_id={"gx": lax.axis_index("gx") + dx, "gy": lax.axis_index("gy") + dy},
            device_id_type=pl.DeviceIdType.MESH,
        )

    for n, (dx, dy) in enumerate(sides):

        @pl.when(jnp.logical_not(inside(-dx, -dy)))
        def _():
            inbox[n] = jnp.zeros(inbox.shape[1:], inbox.dtype)

    grid[...] = jnp.zeros(grid.shape, grid.dtype)
    greet(sides)
    for n, (dx, dy) in enumerate(sides):

        @pl.when(inside(dx, dy))
        def _():
            copy(n).start()

    for n, (dx, dy) in enumerate(sides):

        @pl.when(inside(-dx, -dy))
        def _():
            copy(n).wait_recv()

    for dy in range(-far_y, far_y + 1):
        row = None
        for dx in range(-far_x, far_x + 1):
            tile = mine[...] if (dx, dy) == (0, 0) else inbox[sides.index((-dx, -dy))]
            shift = (dx + far_x) * grid_x
            tile = pltpu.roll(tile, shift, 1) if shift else tile
            row = tile if row is None else row + tile
        top = (dy + far_y) * grid_y
        for c in range(4):
            grid[c, top : top + grid_y, :] = row[c * grid_y : (c + 1) * grid_y]

    y = lax.broadcasted_iota(jnp.int32, (tall, wide), 0)
    x = lax.broadcasted_iota(jnp.int32, (tall, wide), 1)
    y = y + (lax.axis_index("gy") - far_y) * grid_y
    x = x + (lax.axis_index("gx") - far_x) * grid_x
    within = (
        (y >= 0)
        & (y < lax.axis_size("gy") * grid_y)
        & (x >= 0)
        & (x < lax.axis_size("gx") * grid_x)
    )
    data = [grid[c] for c in range(3)]
    mask = grid[3]
    u = [mask * d for d in data]
    for _ in range(SWEEPS):
        east = [pltpu.roll(a, wide - 1, 1) for a in u]
        west = [pltpu.roll(a, 1, 1) for a in u]
        north = [pltpu.roll(a, tall - 1, 0) for a in u]
        south = [pltpu.roll(a, 1, 0) for a in u]
        ahead = [n - s for n, s in zip(north, south)]
        cross = [pltpu.roll(a, wide - 1, 1) - pltpu.roll(a, 1, 1) for a in ahead]
        x_xi = spacing + 0.5 * (east[0] - west[0])
        y_xi = 0.5 * (east[1] - west[1])
        x_eta = 0.5 * ahead[0]
        y_eta = spacing + 0.5 * ahead[1]
        alpha = x_eta * x_eta + y_eta * y_eta
        beta = x_xi * x_eta + y_xi * y_eta
        gamma = x_xi * x_xi + y_xi * y_xi
        new = []
        for c in range(3):
            smooth = (
                alpha * (east[c] + west[c]) + gamma * (north[c] + south[c]) - 0.5 * beta * cross[c]
            ) / (2.0 * (alpha + gamma))
            moved = smooth + 0.5 * mask * (data[c] - smooth)
            new.append(jnp.where(within, moved, 0.0))
        u = new
    top, left = far_y * grid_y, far_x * grid_x
    for c in range(3):
        out[c] = pltpu.roll(u[c], wide - left, 1)[top : top + grid_y, :grid_x]

    for n, (dx, dy) in enumerate(sides):

        @pl.when(inside(dx, dy))
        def _():
            copy(n).wait_send()


def phases(offset, length):
    counter = jnp.arange(length, dtype=jnp.int32)
    shifts = offset[..., None] + jnp.arange(3, dtype=jnp.int32) - 1
    product = jnp.mod(shifts[..., None] * counter, length)
    angle = product.astype(jnp.float32) * (2.0 * math.pi / length)
    return (jnp.cos(angle).astype(jnp.bfloat16), jnp.sin(angle).astype(jnp.bfloat16))


def body(volumes, peaks, valid):
    length = volumes.shape[1]
    margin = length // 4
    stride = length // 2
    half = length // 2 + 1
    _, grid_y, grid_x = peaks.shape
    lanes = grid_x * length
    tall, own = volumes.shape[2:]
    height = tall + 2 * margin
    table_x, table_y, table_z = tables(length, grid_x, grid_y)
    cosine, sine = phases(peaks, length)
    cos_z, sin_z = cosine[2], sine[2]
    rows_re = jnp.concatenate([cos_z, -sin_z], axis=-1)
    rows_im = jnp.concatenate([sin_z, cos_z], axis=-1)
    table_e = jnp.stack([rows_re, rows_im], axis=3).reshape(grid_y, grid_x, 6, 2 * length)
    table_e = jnp.pad(table_e, ((0, 0), (0, 0), (0, 2), (0, 0))).reshape(
        grid_y, grid_x * 8, 2 * length
    )
    weight = np.full((half,), 2.0, np.float32)
    weight[0] = weight[-1] = 1.0

    def spread(table):
        table = table[..., :half].astype(jnp.float32) * weight
        table = jnp.broadcast_to(
            table.transpose(0, 2, 3, 1)[..., None], (grid_y, 3, half, grid_x, length)
        )
        return table.reshape(grid_y, 3, half, lanes)

    sums = pl.pallas_call(
        functools.partial(spectrum_kernel, grid_x, grid_y),
        out_shape=jax.ShapeDtypeStruct((grid_y, 6, 8, lanes), jnp.float32),
        in_specs=[pl.BlockSpec(memory_space=pltpu.VMEM)] * 9,
        out_specs=pl.BlockSpec(memory_space=pltpu.VMEM),
        scratch_shapes=[
            pltpu.VMEM((2, ZSTEP * height, 2 * lanes), jnp.bfloat16),
            pltpu.VMEM((2 * lanes // 128, table_y.shape[0] // 2 * PITCH, 128), jnp.float32),
            pltpu.VMEM((2, length // GROUP, 2, tall, GROUP * margin), jnp.bfloat16),
            pltpu.VMEM((2, 2, length, margin, own), jnp.bfloat16),
            pltpu.VMEM((2, length // GROUP, 2, height, GROUP * margin), jnp.bfloat16),
            pltpu.VMEM((2, length, height, own), jnp.bfloat16),
            pltpu.SemaphoreType.DMA((len(SIDES), PARTS)),
            pltpu.SemaphoreType.DMA((len(SIDES), PARTS)),
        ],
        compiler_params=pltpu.CompilerParams(
            vmem_limit_bytes=56 * 1024 * 1024, collective_id=0, has_side_effects=True
        ),
        name="spectrum",
    )(volumes, *strip_tables(margin, own), table_x, table_y, table_z, table_e, spread(cosine[1]), spread(sine[1]))

    sums = sums.reshape(grid_y, 3, 2, 8, grid_x, length)
    factor = 1.0 / (length * math.sqrt(length))
    cos_x = cosine[0].astype(jnp.float32) * factor
    sin_x = sine[0].astype(jnp.float32) * factor

    def corr(ox, oy, oz):
        real = sums[:, oy, 0, 2 * oz] - sums[:, oy, 1, 2 * oz + 1]
        imag = sums[:, oy, 1, 2 * oz] + sums[:, oy, 0, 2 * oz + 1]
        return jnp.sum(real * cos_x[:, :, ox] - imag * sin_x[:, :, ox], axis=-1)

    centre = corr(1, 1, 1)
    lower = jnp.stack([corr(0, 1, 1), corr(1, 0, 1), corr(1, 1, 0)])
    upper = jnp.stack([corr(2, 1, 1), corr(1, 2, 1), corr(1, 1, 2)])
    shift = jnp.tanh((lower - upper) / (jnp.abs(lower + upper - 2.0 * centre) + 0.5))
    data = peaks.astype(jnp.float32) + shift
    mask = valid.astype(jnp.float32)
    far_x, far_y = reach_of(grid_x, grid_y)
    tall = -(-(2 * far_y + 1) * grid_y // 8) * 8
    wide = -(-(2 * far_x + 1) * grid_x // 128) * 128
    mine = jnp.concatenate([data, mask[None]]).reshape(4 * grid_y, grid_x)
    mine = jnp.pad(mine, ((0, 0), (0, wide - grid_x)))
    count = len(partners(grid_x, grid_y))
    moved = pl.pallas_call(
        functools.partial(sweep_kernel, grid_x, grid_y, float(stride)),
        out_shape=jax.ShapeDtypeStruct(data.shape, jnp.float32),
        in_specs=[pl.BlockSpec(memory_space=pltpu.VMEM)],
        out_specs=pl.BlockSpec(memory_space=pltpu.VMEM),
        scratch_shapes=[
            pltpu.VMEM((count, 4 * grid_y, wide), jnp.float32),
            pltpu.VMEM((4, tall, wide), jnp.float32),
            pltpu.SemaphoreType.DMA((count,)),
            pltpu.SemaphoreType.DMA((count,)),
        ],
        compiler_params=pltpu.CompilerParams(collective_id=1, has_side_effects=True),
        name="sweeps",
    )(mine)
    return (moved, centre)


def solution(mesh):
    return jax.shard_map(
        body,
        mesh=mesh,
        in_specs=(P(None, None, "gy", "gx"), P(None, "gy", "gx"), P("gy", "gx")),
        out_specs=(P(None, "gy", "gx"), P("gy", "gx")),
        check_vma=False,
    )
```

```python
import functools
import math

import jax
import jax.numpy as jnp
import ml_dtypes
import numpy as np
from jax import lax
from jax.experimental import pallas as pl
from jax.experimental.pallas import tpu as pltpu
from jax.sharding import PartitionSpec as P

SWEEPS = 3
ZSTEP = 4
LINES = 3


PARTS = 4
GROUP = 8
PITCH = 136
SIDES = [(dx, dy) for dy in (-1, 0, 1) for dx in (-1, 0, 1) if (dx, dy) != (0, 0)]


def tables(length, grid_x, grid_y):
    counter = np.arange(length)
    angle = (counter[:, None] * counter[None, :] % length).astype(np.float32) * np.float32(
        2.0 * math.pi / length
    )
    factor = np.float32(1.0 / math.sqrt(length))
    cosine = (np.cos(angle) * factor).astype(ml_dtypes.bfloat16)
    sine = (np.sin(angle) * factor).astype(ml_dtypes.bfloat16)
    stride = length // 2
    half = length // 2 + 1
    width = stride * grid_x + stride
    height = stride * grid_y + stride
    along_x = np.zeros((width, 2, grid_x, length), ml_dtypes.bfloat16)
    for i in range(grid_x):
        along_x[i * stride : i * stride + length, 0, i] = cosine
        along_x[i * stride : i * stride + length, 1, i] = -sine
    lines = grid_y * half
    padded = -(-lines // 8) * 8
    along_y = np.zeros((2, padded, 2, height), ml_dtypes.bfloat16)
    for j in range(grid_y):
        rows = slice(j * half, (j + 1) * half)
        window = slice(j * stride, j * stride + length)
        along_y[0, rows, 0, window] = cosine[:half]
        along_y[0, rows, 1, window] = sine[:half]
        along_y[1, rows, 0, window] = -sine[:half]
        along_y[1, rows, 1, window] = cosine[:half]
    along_z = np.block([[cosine, sine], [-sine, cosine]])
    margin = stride // 2
    own = width - 2 * margin
    along_x = along_x.reshape(width, 2 * grid_x * length)
    order = np.zeros((2 * own, along_x.shape[1]), ml_dtypes.bfloat16)
    order[:own] = along_x[margin : margin + own]
    order[own : own + margin] = along_x[:margin]
    order[own + margin : own + 2 * margin] = along_x[margin + own :]
    return (
        order,
        along_y.reshape(2 * padded, 2 * height),
        along_z,
    )


def strip_tables(margin, own):
    pack = np.zeros((GROUP, own, 2, GROUP, margin), ml_dtypes.bfloat16)
    unpack = np.zeros((2, GROUP, margin, GROUP, own), ml_dtypes.bfloat16)
    for g in range(GROUP):
        for m in range(margin):
            pack[g, m, 0, g, m] = 1
            pack[g, own - margin + m, 1, g, m] = 1
            unpack[0, g, m, g, m] = 1
            unpack[1, g, m, g, margin + m] = 1
    return (
        pack.reshape(GROUP * own, 2 * GROUP * margin),
        unpack.reshape(2 * GROUP * margin, GROUP * own),
    )


def inside(dx, dy):
    x = lax.axis_index("gx") + dx
    y = lax.axis_index("gy") + dy
    return (x >= 0) & (x < lax.axis_size("gx")) & (y >= 0) & (y < lax.axis_size("gy"))


def greet(sides):
    barrier = pltpu.get_barrier_semaphore()
    for dx, dy in sides:

        @pl.when(inside(dx, dy))
        def _():
            pl.semaphore_signal(
                barrier,
                inc=1,
                device_id={"gx": lax.axis_index("gx") + dx, "gy": lax.axis_index("gy") + dy},
                device_id_type=pl.DeviceIdType.MESH,
            )

    pl.semaphore_wait(barrier, sum(inside(dx, dy).astype(jnp.int32) for dx, dy in sides))


def reach_of(grid_x, grid_y):
    far_x, far_y = -(-SWEEPS // grid_x), -(-SWEEPS // grid_y)
    return far_x, far_y


def partners(grid_x, grid_y):
    far_x, far_y = reach_of(grid_x, grid_y)
    return [
        (dx, dy)
        for dy in range(-far_y, far_y + 1)
        for dx in range(-far_x, far_x + 1)
        if (dx, dy) != (0, 0)
    ]


def sweep(grid_x, grid_y, spacing, mine, out, inbox, grid, send_sem, recv_sem):
    sides = partners(grid_x, grid_y)
    far_x, far_y = reach_of(grid_x, grid_y)
    tall, wide = grid.shape[1:]

    def copy(n):
        dx, dy = sides[n]
        return pltpu.make_async_remote_copy(
            src_ref=mine,
            dst_ref=inbox.at[n],
            send_sem=send_sem.at[n],
            recv_sem=recv_sem.at[n],
            device_id={"gx": lax.axis_index("gx") + dx, "gy": lax.axis_index("gy") + dy},
            device_id_type=pl.DeviceIdType.MESH,
        )

    for n, (dx, dy) in enumerate(sides):

        @pl.when(inside(dx, dy))
        def _():
            copy(n).start()

    for n, (dx, dy) in enumerate(sides):

        @pl.when(inside(-dx, -dy))
        def _():
            copy(n).wait_recv()

    for dy in range(-far_y, far_y + 1):
        row = None
        for dx in range(-far_x, far_x + 1):
            tile = mine[...] if (dx, dy) == (0, 0) else inbox[sides.index((-dx, -dy))]
            shift = (dx + far_x) * grid_x
            tile = pltpu.roll(tile, shift, 1) if shift else tile
            row = tile if row is None else row + tile
        top = (dy + far_y) * grid_y
        for c in range(4):
            grid[c, top : top + grid_y, :] = row[c * grid_y : (c + 1) * grid_y]

    y = lax.broadcasted_iota(jnp.int32, (tall, wide), 0)
    x = lax.broadcasted_iota(jnp.int32, (tall, wide), 1)
    y = y + (lax.axis_index("gy") - far_y) * grid_y
    x = x + (lax.axis_index("gx") - far_x) * grid_x
    within = (
        (y >= 0)
        & (y < lax.axis_size("gy") * grid_y)
        & (x >= 0)
        & (x < lax.axis_size("gx") * grid_x)
    )
    data = [grid[c] for c in range(3)]
    mask = grid[3]
    u = [mask * d for d in data]
    for _ in range(SWEEPS):
        east = [pltpu.roll(a, wide - 1, 1) for a in u]
        west = [pltpu.roll(a, 1, 1) for a in u]
        north = [pltpu.roll(a, tall - 1, 0) for a in u]
        south = [pltpu.roll(a, 1, 0) for a in u]
        ahead = [n - s for n, s in zip(north, south)]
        cross = [pltpu.roll(a, wide - 1, 1) - pltpu.roll(a, 1, 1) for a in ahead]
        x_xi = spacing + 0.5 * (east[0] - west[0])
        y_xi = 0.5 * (east[1] - west[1])
        x_eta = 0.5 * ahead[0]
        y_eta = spacing + 0.5 * ahead[1]
        alpha = x_eta * x_eta + y_eta * y_eta
        beta = x_xi * x_eta + y_xi * y_eta
        gamma = x_xi * x_xi + y_xi * y_xi
        new = []
        for c in range(3):
            smooth = (
                alpha * (east[c] + west[c]) + gamma * (north[c] + south[c]) - 0.5 * beta * cross[c]
            ) / (2.0 * (alpha + gamma))
            moved = smooth + 0.5 * mask * (data[c] - smooth)
            new.append(jnp.where(within, moved, 0.0))
        u = new
    top, left = far_y * grid_y, far_x * grid_x
    for c in range(3):
        out[c] = pltpu.roll(u[c], wide - left, 1)[top : top + grid_y, :grid_x]

    for n, (dx, dy) in enumerate(sides):

        @pl.when(inside(dx, dy))
        def _():
            copy(n).wait_send()


def clear_inbox(grid_x, grid_y, inbox, grid):
    for n, (dx, dy) in enumerate(partners(grid_x, grid_y)):

        @pl.when(jnp.logical_not(inside(-dx, -dy)))
        def _():
            inbox[n] = jnp.zeros(inbox.shape[1:], inbox.dtype)

    grid[...] = jnp.zeros(grid.shape, grid.dtype)


def turn(count, length):
    def wave(steps):
        y = (jnp.abs(steps - length // 2) - length // 4).astype(jnp.float32)
        y = y * (2.0 * math.pi / length)
        t = y * y
        value = -1.0 / 39916800.0
        for term in (1.0 / 362880.0, -1.0 / 5040.0, 1.0 / 120.0, -1.0 / 6.0, 1.0):
            value = value * t + term
        return (value * y).astype(jnp.bfloat16).astype(jnp.float32)

    whole = length - 1
    return wave(count & whole), wave((count - length // 4) & whole)


def phase_tables(grid_x, grid_y, length, peaks, table_e, cos_y, sin_y):
    half = length // 2 + 1
    lines, lanes = cos_y.shape[2:]
    own = lax.broadcasted_iota(jnp.int32, (lines, lanes), 1) // length
    k = lax.broadcasted_iota(jnp.int32, (lines, lanes), 0)
    weight = jnp.where((k == 0) | (k == half - 1), 1.0, 2.0)
    row = lax.broadcasted_iota(jnp.int32, table_e.shape[1:], 0)
    lane = lax.broadcasted_iota(jnp.int32, table_e.shape[1:], 1)
    outer, inner = row & 1, lane // length
    for j in range(grid_y):
        peak = jnp.zeros((lines, lanes), jnp.int32)
        deep = jnp.zeros(table_e.shape[1:], jnp.int32)
        for i in range(grid_x):
            peak = jnp.where(own == i, peaks[1, j, i], peak)
            deep = jnp.where(row // 8 == i, peaks[2, j, i], deep)
        for o in range(3):
            cosine, sine = turn((peak + (o - 1)) * k, length)
            cos_y[j, o] = cosine * weight
            sin_y[j, o] = sine * weight
        offset = deep + (row & 7) // 2 - 1
        cosine, sine = turn(offset * (lane & (length - 1)), length)
        signed = jnp.where(outer == 0, -sine, sine)
        table_e[j] = jnp.where(outer == inner, cosine, signed).astype(jnp.bfloat16)


def measure_peaks(grid_x, grid_y, length, peaks, valid, sums, group, mine, score):
    lanes = group.shape[1]
    wide = mine.shape[1]
    k = lax.broadcasted_iota(jnp.int32, (8, lanes), 1) & (length - 1)
    o = lax.broadcasted_iota(jnp.int32, (8, lanes), 0)
    column = lax.broadcasted_iota(jnp.int32, (8, wide), 1)
    line = lax.broadcasted_iota(jnp.int32, (8, wide), 0)
    factor = 1.0 / (length * math.sqrt(length))
    for j in range(grid_y):
        peak = jnp.zeros((8, lanes), jnp.int32)
        for i in range(grid_x):
            peak = jnp.where(group == i, peaks[0, j, i], peak)
        cos_x, sin_x = turn((peak + (o - 1)) * k, length)

        def corr(ox, oy, oz):
            by_cos, by_sin = sums[j][2 * oy], sums[j][2 * oy + 1]
            re, im = slice(2 * oz, 2 * oz + 1), slice(2 * oz + 1, 2 * oz + 2)
            real = by_cos[re] - by_sin[im]
            imag = by_sin[re] + by_cos[im]
            return real * cos_x[ox : ox + 1] - imag * sin_x[ox : ox + 1]

        spots = [(1, 1, 1), (0, 1, 1), (1, 0, 1), (1, 1, 0), (2, 1, 1), (1, 2, 1), (1, 1, 2)]
        rows = [corr(*spot) for spot in spots]
        rows = jnp.concatenate(rows + [jnp.zeros_like(rows[0])], axis=0)
        cube = jnp.zeros((8, wide), jnp.float32)
        start = jnp.zeros((8, wide), jnp.float32)
        trust = jnp.zeros((8, wide), jnp.float32)
        for i in range(grid_x):
            total = jnp.sum(jnp.where(group == i, rows, 0.0), axis=1, keepdims=True)
            cube = jnp.where(column == i, total * factor, cube)
            trust = jnp.where(column == i, valid[j, i].astype(jnp.float32), trust)
            for c in range(3):
                here = (column == i) & (line == c)
                start = jnp.where(here, peaks[c, j, i].astype(jnp.float32), start)
        centre = cube[0:1]
        lower, upper = cube[1:4], cube[4:7]
        shift = jnp.tanh((lower - upper) / (jnp.abs(lower + upper - 2.0 * centre) + 0.5))
        data = start[:3] + shift
        for c in range(3):
            mine[c * grid_y + j : c * grid_y + j + 1, :] = data[c : c + 1]
        mine[3 * grid_y + j : 3 * grid_y + j + 1, :] = trust[:1]
        score[j : j + 1, :] = centre[:, :grid_x]


def spectrum_kernel(
    grid_x,
    grid_y,
    vol,
    pack,
    unpack,
    table_x,
    table_y,
    table_z,
    peaks,
    valid,
    moved,
    score,
    table_e,
    cos_y,
    sin_y,
    first,
    second,
    strip,
    side_y,
    side_x,
    margins,
    send_sem,
    recv_sem,
    mine,
    inbox,
    grid,
    sweep_send,
    sweep_recv,
):
    length = vol.shape[1]
    tall = vol.shape[2]
    own = vol.shape[3]
    margin = length // 4
    height = tall + 2 * margin
    depth = length // PARTS
    chunks = depth // GROUP

    def copy(dx, dy, part):
        rows = {-1: pl.ds(0, margin), 0: pl.ds(0, tall), 1: pl.ds(tall - margin, margin)}[dy]
        if dx == 0:
            zs = pl.ds(part * depth, depth)
            src = vol.at[:, zs, rows, :]
            dst = side_y.at[(1 - dy) // 2, :, zs, :, :]
        else:
            cs = pl.ds(part * chunks, chunks)
            to = {
                1: pl.ds(0, margin),
                0: pl.ds(margin, tall),
                -1: pl.ds(tall + margin, margin),
            }[dy]
            src = strip.at[(1 + dx) // 2, cs, :, rows, :]
            dst = side_x.at[(1 - dx) // 2, cs, :, to, :]
        n = SIDES.index((dx, dy))
        return pltpu.make_async_remote_copy(
            src_ref=src,
            dst_ref=dst,
            send_sem=send_sem.at[n, part],
            recv_sem=recv_sem.at[n, part],
            device_id={"gx": lax.axis_index("gx") + dx, "gy": lax.axis_index("gy") + dy},
            device_id_type=pl.DeviceIdType.MESH,
        )

    for side, (dx, dy) in enumerate(((0, -1), (0, 1))):

        @pl.when(jnp.logical_not(inside(dx, dy)))
        def _():
            side_y[side] = jnp.zeros(side_y.shape[1:], side_y.dtype)

    for side, dx in enumerate((-1, 1)):
        for dy, lo, count in ((-1, 0, margin), (0, margin, tall), (1, margin + tall, margin)):

            @pl.when(jnp.logical_not(inside(dx, dy)))
            def _():
                side_x[side, :, :, lo : lo + count, :] = jnp.zeros(
                    (side_x.shape[1], 2, count, side_x.shape[4]), side_x.dtype
                )

    clear_inbox(grid_x, grid_y, inbox, grid)
    greet(partners(grid_x, grid_y))

    def send_strips(part, carry):
        for dx, dy in SIDES:
            if dx == 0:

                @pl.when(inside(dx, dy))
                def _():
                    copy(dx, dy, part).start()

        for i in range(chunks):
            c = part * chunks + i
            wide = jnp.concatenate(
                [vol[:, c * GROUP + g].reshape(2 * tall, own) for g in range(GROUP)], axis=1
            )
            packed = jnp.dot(wide, pack[...], preferred_element_type=jnp.float32)
            packed = packed.astype(jnp.bfloat16).reshape(2, tall, 2 * GROUP * margin)
            strip[0, c] = packed[:, :, : GROUP * margin]
            strip[1, c] = packed[:, :, GROUP * margin :]
        for dx, dy in SIDES:
            if dx != 0:

                @pl.when(inside(dx, dy))
                def _():
                    copy(dx, dy, part).start()

        return carry

    lax.fori_loop(0, PARTS, send_strips, 0)

    half = length // 2 + 1
    lanes = grid_x * length
    padded = table_y.shape[0] // 2
    pieces = 2 * lanes // 128

    group = lax.broadcasted_iota(jnp.int32, (8, lanes), 1) // length
    phase_tables(grid_x, grid_y, length, peaks, table_e, cos_y, sin_y)

    def widen(part, lo, count):
        for i in range(chunks):
            c = part * chunks + i
            wide = jnp.concatenate(
                [
                    side_x[s, c, :, lo : lo + count, :].reshape(2 * count, GROUP * margin)
                    for s in range(2)
                ],
                axis=1,
            )
            apart = jnp.dot(wide, unpack[...], preferred_element_type=jnp.float32)
            apart = apart.astype(jnp.bfloat16).reshape(2, count, GROUP * own)
            for g in range(GROUP):
                margins[:, c * GROUP + g, lo : lo + count, :] = apart[
                    :, :, g * own : (g + 1) * own
                ]

    def along_x(v, zs, rows, lo, count):
        rows = jnp.concatenate([rows, margins[v, zs, lo : lo + count, :]], axis=2)
        rows = rows.reshape(ZSTEP * count, 2 * own)
        one = jnp.dot(rows, table_x[...], preferred_element_type=jnp.float32)
        one = one.astype(jnp.bfloat16).reshape(ZSTEP, count, 2 * lanes)
        first[v, zs, lo : lo + count, :] = one

    steps = depth // ZSTEP

    def take_middle(part, carry):
        for dx, dy in SIDES:
            if dy == 0:

                @pl.when(inside(-dx, -dy))
                def _():
                    copy(dx, dy, part).wait_recv()

        widen(part, margin, tall)

        def middle(step, carry):
            zs = pl.ds(step * ZSTEP, ZSTEP)
            for v in range(2):
                along_x(v, zs, vol[v, zs], margin, tall)
            return carry

        return lax.fori_loop(part * steps, (part + 1) * steps, middle, carry)

    lax.fori_loop(0, PARTS, take_middle, 0)

    def slab(step, carry):
        z0 = step * ZSTEP
        zs = pl.ds(z0, ZSTEP)
        for v in range(2):
            along_x(v, zs, side_y[0, v, zs], 0, margin)
            along_x(v, zs, side_y[1, v, zs], margin + tall, margin)
        for i in range(ZSTEP):
            z = z0 + i
            right = jnp.concatenate(
                [
                    jnp.concatenate([first[0, z, :, :lanes], first[1, z, :, :lanes]], axis=1),
                    jnp.concatenate([first[0, z, :, lanes:], first[1, z, :, lanes:]], axis=1),
                ],
                axis=0,
            )
            two = jnp.dot(table_y[...], right, preferred_element_type=jnp.float32)
            for c in range(2):
                for t in range(pieces):
                    second[t, pl.ds(c * length + z, padded, stride=PITCH), :] = two[
                        c * padded : (c + 1) * padded, t * 128 : (t + 1) * 128
                    ]
        return carry

    def take_ends(part, carry):
        for dx, dy in SIDES:
            if dy != 0:

                @pl.when(inside(-dx, -dy))
                def _():
                    copy(dx, dy, part).wait_recv()

        widen(part, 0, margin)
        widen(part, margin + tall, margin)
        return lax.fori_loop(part * steps, (part + 1) * steps, slab, carry)

    lax.fori_loop(0, PARTS, take_ends, 0)

    def one_line(j, ky, sums):
        base = pl.multiple_of((j * half + ky) * PITCH, 8)
        right = jnp.concatenate(
            [second[t, pl.ds(base, 2 * length), :].astype(jnp.bfloat16) for t in range(pieces)],
            axis=1,
        )
        three = jnp.dot(table_z[...], right, preferred_element_type=jnp.float32)
        re1, im1 = three[:length, :lanes], three[length:, :lanes]
        re2, im2 = three[:length, lanes:], three[length:, lanes:]
        size = (re1 * re1 + im1 * im1) * (re2 * re2 + im2 * im2)
        scale = 1.0 / (jnp.sqrt(size) + 1.0)
        real_r = ((re1 * re2 + im1 * im2) * scale).astype(jnp.bfloat16)
        imag_r = ((im1 * re2 - re1 * im2) * scale).astype(jnp.bfloat16)
        both = jnp.concatenate([real_r, imag_r], axis=0)
        along = jnp.dot(table_e[j], both, preferred_element_type=jnp.float32)
        own_rows = along[:8]
        for i in range(1, grid_x):
            own_rows = jnp.where(group == i, along[8 * i : 8 * i + 8], own_rows)
        new = []
        for o in range(3):
            new.append(sums[2 * o] + own_rows * cos_y[j, o, pl.ds(ky, 1), :])
            new.append(sums[2 * o + 1] + own_rows * sin_y[j, o, pl.ds(ky, 1), :])
        return tuple(new)

    def line(step, sums):
        for i in range(LINES):
            ky = step * LINES + i
            sums = tuple(one_line(j, ky, sums[j]) for j in range(grid_y))
        return sums

    zero = jnp.zeros((8, lanes), jnp.float32)
    sums = lax.fori_loop(0, half // LINES, line, ((zero,) * 6,) * grid_y)
    for i in range(half // LINES * LINES, half):
        sums = tuple(one_line(j, i, sums[j]) for j in range(grid_y))
    measure_peaks(grid_x, grid_y, length, peaks, valid, sums, group, mine, score)
    sweep(grid_x, grid_y, float(length // 2), mine, moved, inbox, grid, sweep_send, sweep_recv)

    def sent(part, carry):
        for dx, dy in SIDES:

            @pl.when(inside(dx, dy))
            def _():
                copy(dx, dy, part).wait_send()

        return carry

    lax.fori_loop(0, PARTS, sent, 0)


def body(volumes, peaks, valid):
    length = volumes.shape[1]
    margin = length // 4
    half = length // 2 + 1
    _, grid_y, grid_x = peaks.shape
    lanes = grid_x * length
    tall, own = volumes.shape[2:]
    height = tall + 2 * margin
    table_x, table_y, table_z = tables(length, grid_x, grid_y)
    far_x, far_y = reach_of(grid_x, grid_y)
    deep = -(-(2 * far_y + 1) * grid_y // 8) * 8
    wide = -(-(2 * far_x + 1) * grid_x // 128) * 128
    lines = -(-half // 8) * 8
    count = len(partners(grid_x, grid_y))
    vmem = pl.BlockSpec(memory_space=pltpu.VMEM)
    smem = pl.BlockSpec(memory_space=pltpu.SMEM)
    return pl.pallas_call(
        functools.partial(spectrum_kernel, grid_x, grid_y),
        out_shape=(
            jax.ShapeDtypeStruct(peaks.shape, jnp.float32),
            jax.ShapeDtypeStruct(valid.shape, jnp.float32),
        ),
        in_specs=[vmem] * 6 + [smem] * 2,
        out_specs=(vmem, vmem),
        scratch_shapes=[
            pltpu.VMEM((grid_y, grid_x * 8, 2 * length), jnp.bfloat16),
            pltpu.VMEM((grid_y, 3, lines, lanes), jnp.float32),
            pltpu.VMEM((grid_y, 3, lines, lanes), jnp.float32),
            pltpu.VMEM((2, length, height, 2 * lanes), jnp.bfloat16),
            pltpu.VMEM((2 * lanes // 128, table_y.shape[0] // 2 * PITCH, 128), jnp.float32),
            pltpu.VMEM((2, length // GROUP, 2, tall, GROUP * margin), jnp.bfloat16),
            pltpu.VMEM((2, 2, length, margin, own), jnp.bfloat16),
            pltpu.VMEM((2, length // GROUP, 2, height, GROUP * margin), jnp.bfloat16),
            pltpu.VMEM((2, length, height, own), jnp.bfloat16),
            pltpu.SemaphoreType.DMA((len(SIDES), PARTS)),
            pltpu.SemaphoreType.DMA((len(SIDES), PARTS)),
            pltpu.VMEM((4 * grid_y, wide), jnp.float32),
            pltpu.VMEM((count, 4 * grid_y, wide), jnp.float32),
            pltpu.VMEM((4, deep, wide), jnp.float32),
            pltpu.SemaphoreType.DMA((count,)),
            pltpu.SemaphoreType.DMA((count,)),
        ],
        compiler_params=pltpu.CompilerParams(
            vmem_limit_bytes=60 * 1024 * 1024, collective_id=0, has_side_effects=True
        ),
        name="correlate",
    )(volumes, *strip_tables(margin, own), table_x, table_y, table_z, peaks, valid)


def solution(mesh):
    return jax.shard_map(
        body,
        mesh=mesh,
        in_specs=(P(None, None, "gy", "gx"), P(None, "gy", "gx"), P("gy", "gx")),
        out_specs=(P(None, "gy", "gx"), P("gy", "gx")),
        check_vma=False,
    )
```

```python
import functools
import math

import jax
import jax.numpy as jnp
import ml_dtypes
import numpy as np
from jax import lax
from jax.experimental import pallas as pl
from jax.experimental.pallas import tpu as pltpu
from jax.sharding import PartitionSpec as P

SWEEPS = 3
ZSTEP = 4
LINES = 3


PARTS = 8
GROUP = 8
PITCH = 136
SIDES = [(dx, dy) for dy in (-1, 0, 1) for dx in (-1, 0, 1) if (dx, dy) != (0, 0)]


def tables(length, grid_x, grid_y):
    counter = np.arange(length)
    angle = (counter[:, None] * counter[None, :] % length).astype(np.float32) * np.float32(
        2.0 * math.pi / length
    )
    factor = np.float32(1.0 / math.sqrt(length))
    cosine = (np.cos(angle) * factor).astype(ml_dtypes.bfloat16)
    sine = (np.sin(angle) * factor).astype(ml_dtypes.bfloat16)
    stride = length // 2
    half = length // 2 + 1
    width = stride * grid_x + stride
    height = stride * grid_y + stride
    along_x = np.zeros((width, 2, grid_x, length), ml_dtypes.bfloat16)
    for i in range(grid_x):
        along_x[i * stride : i * stride + length, 0, i] = cosine
        along_x[i * stride : i * stride + length, 1, i] = -sine
    lines = grid_y * half
    padded = -(-lines // 8) * 8
    along_y = np.zeros((2, padded, 2, height), ml_dtypes.bfloat16)
    for j in range(grid_y):
        rows = slice(j * half, (j + 1) * half)
        window = slice(j * stride, j * stride + length)
        along_y[0, rows, 0, window] = cosine[:half]
        along_y[0, rows, 1, window] = sine[:half]
        along_y[1, rows, 0, window] = -sine[:half]
        along_y[1, rows, 1, window] = cosine[:half]
    along_z = np.block([[cosine, sine], [-sine, cosine]])
    margin = stride // 2
    own = width - 2 * margin
    along_x = along_x.reshape(width, 2 * grid_x * length)
    order = np.zeros((2 * own, along_x.shape[1]), ml_dtypes.bfloat16)
    order[:own] = along_x[margin : margin + own]
    order[own : own + margin] = along_x[:margin]
    order[own + margin : own + 2 * margin] = along_x[margin + own :]
    return (
        order,
        along_y.reshape(2 * padded, 2 * height),
        along_z,
    )


def strip_tables(margin, own):
    pack = np.zeros((GROUP, own, 2, GROUP, margin), ml_dtypes.bfloat16)
    unpack = np.zeros((2, GROUP, margin, GROUP, own), ml_dtypes.bfloat16)
    for g in range(GROUP):
        for m in range(margin):
            pack[g, m, 0, g, m] = 1
            pack[g, own - margin + m, 1, g, m] = 1
            unpack[0, g, m, g, m] = 1
            unpack[1, g, m, g, margin + m] = 1
    return (
        pack.reshape(GROUP * own, 2 * GROUP * margin),
        unpack.reshape(2 * GROUP * margin, GROUP * own),
    )


def inside(dx, dy):
    x = lax.axis_index("gx") + dx
    y = lax.axis_index("gy") + dy
    return (x >= 0) & (x < lax.axis_size("gx")) & (y >= 0) & (y < lax.axis_size("gy"))


def greet(sides):
    barrier = pltpu.get_barrier_semaphore()
    for dx, dy in sides:

        @pl.when(inside(dx, dy))
        def _():
            pl.semaphore_signal(
                barrier,
                inc=1,
                device_id={"gx": lax.axis_index("gx") + dx, "gy": lax.axis_index("gy") + dy},
                device_id_type=pl.DeviceIdType.MESH,
            )

    pl.semaphore_wait(barrier, sum(inside(dx, dy).astype(jnp.int32) for dx, dy in sides))


def reach_of(grid_x, grid_y):
    far_x, far_y = -(-SWEEPS // grid_x), -(-SWEEPS // grid_y)
    return far_x, far_y


def partners(grid_x, grid_y):
    far_x, far_y = reach_of(grid_x, grid_y)
    return [
        (dx, dy)
        for dy in range(-far_y, far_y + 1)
        for dx in range(-far_x, far_x + 1)
        if (dx, dy) != (0, 0)
    ]


def sweep(grid_x, grid_y, spacing, mine, out, inbox, grid, send_sem, recv_sem):
    sides = partners(grid_x, grid_y)
    far_x, far_y = reach_of(grid_x, grid_y)
    tall, wide = grid.shape[1:]

    def copy(n):
        dx, dy = sides[n]
        return pltpu.make_async_remote_copy(
            src_ref=mine,
            dst_ref=inbox.at[n],
            send_sem=send_sem.at[n],
            recv_sem=recv_sem.at[n],
            device_id={"gx": lax.axis_index("gx") + dx, "gy": lax.axis_index("gy") + dy},
            device_id_type=pl.DeviceIdType.MESH,
        )

    for n, (dx, dy) in enumerate(sides):

        @pl.when(inside(dx, dy))
        def _():
            copy(n).start()

    for n, (dx, dy) in enumerate(sides):

        @pl.when(inside(-dx, -dy))
        def _():
            copy(n).wait_recv()

    for dy in range(-far_y, far_y + 1):
        row = None
        for dx in range(-far_x, far_x + 1):
            tile = mine[...] if (dx, dy) == (0, 0) else inbox[sides.index((-dx, -dy))]
            shift = (dx + far_x) * grid_x
            tile = pltpu.roll(tile, shift, 1) if shift else tile
            row = tile if row is None else row + tile
        top = (dy + far_y) * grid_y
        for c in range(4):
            grid[c, top : top + grid_y, :] = row[c * grid_y : (c + 1) * grid_y]

    y = lax.broadcasted_iota(jnp.int32, (tall, wide), 0)
    x = lax.broadcasted_iota(jnp.int32, (tall, wide), 1)
    y = y + (lax.axis_index("gy") - far_y) * grid_y
    x = x + (lax.axis_index("gx") - far_x) * grid_x
    within = (
        (y >= 0)
        & (y < lax.axis_size("gy") * grid_y)
        & (x >= 0)
        & (x < lax.axis_size("gx") * grid_x)
    )
    data = [grid[c] for c in range(3)]
    mask = grid[3]
    u = [mask * d for d in data]
    for _ in range(SWEEPS):
        east = [pltpu.roll(a, wide - 1, 1) for a in u]
        west = [pltpu.roll(a, 1, 1) for a in u]
        north = [pltpu.roll(a, tall - 1, 0) for a in u]
        south = [pltpu.roll(a, 1, 0) for a in u]
        ahead = [n - s for n, s in zip(north, south)]
        cross = [pltpu.roll(a, wide - 1, 1) - pltpu.roll(a, 1, 1) for a in ahead]
        x_xi = spacing + 0.5 * (east[0] - west[0])
        y_xi = 0.5 * (east[1] - west[1])
        x_eta = 0.5 * ahead[0]
        y_eta = spacing + 0.5 * ahead[1]
        alpha = x_eta * x_eta + y_eta * y_eta
        beta = x_xi * x_eta + y_xi * y_eta
        gamma = x_xi * x_xi + y_xi * y_xi
        new = []
        for c in range(3):
            smooth = (
                alpha * (east[c] + west[c]) + gamma * (north[c] + south[c]) - 0.5 * beta * cross[c]
            ) / (2.0 * (alpha + gamma))
            moved = smooth + 0.5 * mask * (data[c] - smooth)
            new.append(jnp.where(within, moved, 0.0))
        u = new
    top, left = far_y * grid_y, far_x * grid_x
    for c in range(3):
        out[c] = pltpu.roll(u[c], wide - left, 1)[top : top + grid_y, :grid_x]

    for n, (dx, dy) in enumerate(sides):

        @pl.when(inside(dx, dy))
        def _():
            copy(n).wait_send()


def clear_inbox(grid_x, grid_y, inbox, grid):
    for n, (dx, dy) in enumerate(partners(grid_x, grid_y)):

        @pl.when(jnp.logical_not(inside(-dx, -dy)))
        def _():
            inbox[n] = jnp.zeros(inbox.shape[1:], inbox.dtype)

    grid[...] = jnp.zeros(grid.shape, grid.dtype)


def turn(count, length):
    def wave(steps):
        y = (jnp.abs(steps - length // 2) - length // 4).astype(jnp.float32)
        y = y * (2.0 * math.pi / length)
        t = y * y
        value = -1.0 / 39916800.0
        for term in (1.0 / 362880.0, -1.0 / 5040.0, 1.0 / 120.0, -1.0 / 6.0, 1.0):
            value = value * t + term
        return (value * y).astype(jnp.bfloat16).astype(jnp.float32)

    whole = length - 1
    return wave(count & whole), wave((count - length // 4) & whole)


def phase_tables(grid_x, grid_y, length, peaks, table_e, cos_y, sin_y):
    half = length // 2 + 1
    lines, lanes = cos_y.shape[2:]
    own = lax.broadcasted_iota(jnp.int32, (lines, lanes), 1) // length
    k = lax.broadcasted_iota(jnp.int32, (lines, lanes), 0)
    weight = jnp.where((k == 0) | (k == half - 1), 1.0, 2.0)
    row = lax.broadcasted_iota(jnp.int32, table_e.shape[1:], 0)
    lane = lax.broadcasted_iota(jnp.int32, table_e.shape[1:], 1)
    outer, inner = row & 1, lane // length
    for j in range(grid_y):
        peak = jnp.zeros((lines, lanes), jnp.int32)
        deep = jnp.zeros(table_e.shape[1:], jnp.int32)
        for i in range(grid_x):
            peak = jnp.where(own == i, peaks[1, j, i], peak)
            deep = jnp.where(row // 8 == i, peaks[2, j, i], deep)
        for o in range(3):
            cosine, sine = turn((peak + (o - 1)) * k, length)
            cos_y[j, o] = cosine * weight
            sin_y[j, o] = sine * weight
        offset = deep + (row & 7) // 2 - 1
        cosine, sine = turn(offset * (lane & (length - 1)), length)
        signed = jnp.where(outer == 0, -sine, sine)
        table_e[j] = jnp.where(outer == inner, cosine, signed).astype(jnp.bfloat16)


def measure_peaks(grid_x, grid_y, length, peaks, valid, sums, group, mine, out):
    lanes = group.shape[1]
    wide = mine.shape[1]
    k = lax.broadcasted_iota(jnp.int32, (8, lanes), 1) & (length - 1)
    o = lax.broadcasted_iota(jnp.int32, (8, lanes), 0)
    column = lax.broadcasted_iota(jnp.int32, (8, wide), 1)
    line = lax.broadcasted_iota(jnp.int32, (8, wide), 0)
    factor = 1.0 / (length * math.sqrt(length))
    for j in range(grid_y):
        peak = jnp.zeros((8, lanes), jnp.int32)
        for i in range(grid_x):
            peak = jnp.where(group == i, peaks[0, j, i], peak)
        cos_x, sin_x = turn((peak + (o - 1)) * k, length)

        def corr(ox, oy, oz):
            by_cos, by_sin = sums[j][2 * oy], sums[j][2 * oy + 1]
            re, im = slice(2 * oz, 2 * oz + 1), slice(2 * oz + 1, 2 * oz + 2)
            real = by_cos[re] - by_sin[im]
            imag = by_sin[re] + by_cos[im]
            return real * cos_x[ox : ox + 1] - imag * sin_x[ox : ox + 1]

        spots = [(1, 1, 1), (0, 1, 1), (1, 0, 1), (1, 1, 0), (2, 1, 1), (1, 2, 1), (1, 1, 2)]
        rows = [corr(*spot) for spot in spots]
        rows = jnp.concatenate(rows + [jnp.zeros_like(rows[0])], axis=0)
        cube = jnp.zeros((8, wide), jnp.float32)
        start = jnp.zeros((8, wide), jnp.float32)
        trust = jnp.zeros((8, wide), jnp.float32)
        for i in range(grid_x):
            total = jnp.sum(jnp.where(group == i, rows, 0.0), axis=1, keepdims=True)
            cube = jnp.where(column == i, total * factor, cube)
            trust = jnp.where(column == i, valid[j, i].astype(jnp.float32), trust)
            for c in range(3):
                here = (column == i) & (line == c)
                start = jnp.where(here, peaks[c, j, i].astype(jnp.float32), start)
        centre = cube[0:1]
        lower, upper = cube[1:4], cube[4:7]
        shift = jnp.tanh((lower - upper) / (jnp.abs(lower + upper - 2.0 * centre) + 0.5))
        data = start[:3] + shift
        for c in range(3):
            mine[c * grid_y + j : c * grid_y + j + 1, :] = data[c : c + 1]
        mine[3 * grid_y + j : 3 * grid_y + j + 1, :] = trust[:1]
        out[3, j : j + 1, :] = centre[:, :grid_x]


def spectrum_kernel(
    grid_x,
    grid_y,
    vol,
    pack,
    unpack,
    table_x,
    table_y,
    table_z,
    peaks,
    valid,
    moved,
    table_e,
    cos_y,
    sin_y,
    first,
    second,
    strip,
    side_y,
    side_x,
    margins,
    send_sem,
    recv_sem,
    mine,
    inbox,
    grid,
    sweep_send,
    sweep_recv,
):
    length = vol.shape[1]
    tall = vol.shape[2]
    own = vol.shape[3]
    margin = length // 4
    height = tall + 2 * margin
    depth = length // PARTS
    chunks = depth // GROUP

    def copy(dx, dy, part):
        rows = {-1: pl.ds(0, margin), 0: pl.ds(0, tall), 1: pl.ds(tall - margin, margin)}[dy]
        if dx == 0:
            zs = pl.ds(part * depth, depth)
            src = vol.at[:, zs, rows, :]
            dst = side_y.at[(1 - dy) // 2, :, zs, :, :]
        else:
            cs = pl.ds(part * chunks, chunks)
            to = {
                1: pl.ds(0, margin),
                0: pl.ds(margin, tall),
                -1: pl.ds(tall + margin, margin),
            }[dy]
            src = strip.at[(1 + dx) // 2, cs, :, rows, :]
            dst = side_x.at[(1 - dx) // 2, cs, :, to, :]
        n = SIDES.index((dx, dy))
        return pltpu.make_async_remote_copy(
            src_ref=src,
            dst_ref=dst,
            send_sem=send_sem.at[n, part],
            recv_sem=recv_sem.at[n, part],
            device_id={"gx": lax.axis_index("gx") + dx, "gy": lax.axis_index("gy") + dy},
            device_id_type=pl.DeviceIdType.MESH,
        )

    for side, (dx, dy) in enumerate(((0, -1), (0, 1))):

        @pl.when(jnp.logical_not(inside(dx, dy)))
        def _():
            side_y[side] = jnp.zeros(side_y.shape[1:], side_y.dtype)

    for side, dx in enumerate((-1, 1)):
        for dy, lo, count in ((-1, 0, margin), (0, margin, tall), (1, margin + tall, margin)):

            @pl.when(jnp.logical_not(inside(dx, dy)))
            def _():
                side_x[side, :, :, lo : lo + count, :] = jnp.zeros(
                    (side_x.shape[1], 2, count, side_x.shape[4]), side_x.dtype
                )

    clear_inbox(grid_x, grid_y, inbox, grid)
    greet(partners(grid_x, grid_y))

    def send_strips(part, carry):
        for dx, dy in SIDES:
            if dx == 0:

                @pl.when(inside(dx, dy))
                def _():
                    copy(dx, dy, part).start()

        for i in range(chunks):
            c = part * chunks + i
            wide = jnp.concatenate(
                [vol[:, c * GROUP + g].reshape(2 * tall, own) for g in range(GROUP)], axis=1
            )
            packed = jnp.dot(wide, pack[...], preferred_element_type=jnp.float32)
            packed = packed.astype(jnp.bfloat16).reshape(2, tall, 2 * GROUP * margin)
            strip[0, c] = packed[:, :, : GROUP * margin]
            strip[1, c] = packed[:, :, GROUP * margin :]
        for dx, dy in SIDES:
            if dx != 0:

                @pl.when(inside(dx, dy))
                def _():
                    copy(dx, dy, part).start()

        return carry

    lax.fori_loop(0, PARTS, send_strips, 0)

    half = length // 2 + 1
    lanes = grid_x * length
    padded = table_y.shape[0] // 2
    pieces = 2 * lanes // 128

    group = lax.broadcasted_iota(jnp.int32, (8, lanes), 1) // length
    phase_tables(grid_x, grid_y, length, peaks, table_e, cos_y, sin_y)

    def widen(part, lo, count):
        for i in range(chunks):
            c = part * chunks + i
            wide = jnp.concatenate(
                [
                    side_x[s, c, :, lo : lo + count, :].reshape(2 * count, GROUP * margin)
                    for s in range(2)
                ],
                axis=1,
            )
            apart = jnp.dot(wide, unpack[...], preferred_element_type=jnp.float32)
            apart = apart.astype(jnp.bfloat16).reshape(2, count, GROUP * own)
            for g in range(GROUP):
                margins[:, c * GROUP + g, lo : lo + count, :] = apart[
                    :, :, g * own : (g + 1) * own
                ]

    def along_x(v, zs, rows, lo, count):
        rows = jnp.concatenate([rows, margins[v, zs, lo : lo + count, :]], axis=2)
        rows = rows.reshape(ZSTEP * count, 2 * own)
        one = jnp.dot(rows, table_x[...], preferred_element_type=jnp.float32)
        one = one.astype(jnp.bfloat16).reshape(ZSTEP, count, 2 * lanes)
        first[v, zs, lo : lo + count, :] = one

    steps = depth // ZSTEP

    def take_middle(part, carry):
        for dx, dy in SIDES:
            if dy == 0:

                @pl.when(inside(-dx, -dy))
                def _():
                    copy(dx, dy, part).wait_recv()

        widen(part, margin, tall)

        def middle(step, carry):
            zs = pl.ds(step * ZSTEP, ZSTEP)
            for v in range(2):
                along_x(v, zs, vol[v, zs], margin, tall)
            return carry

        return lax.fori_loop(part * steps, (part + 1) * steps, middle, carry)

    lax.fori_loop(0, PARTS, take_middle, 0)

    def slab(step, carry):
        z0 = step * ZSTEP
        zs = pl.ds(z0, ZSTEP)
        for v in range(2):
            along_x(v, zs, side_y[0, v, zs], 0, margin)
            along_x(v, zs, side_y[1, v, zs], margin + tall, margin)
        for i in range(ZSTEP):
            z = z0 + i
            right = jnp.concatenate(
                [
                    jnp.concatenate([first[0, z, :, :lanes], first[1, z, :, :lanes]], axis=1),
                    jnp.concatenate([first[0, z, :, lanes:], first[1, z, :, lanes:]], axis=1),
                ],
                axis=0,
            )
            two = jnp.dot(table_y[...], right, preferred_element_type=jnp.float32)
            for c in range(2):
                for t in range(pieces):
                    second[t, pl.ds(c * length + z, padded, stride=PITCH), :] = two[
                        c * padded : (c + 1) * padded, t * 128 : (t + 1) * 128
                    ]
        return carry

    def take_ends(part, carry):
        for dx, dy in SIDES:
            if dy != 0:

                @pl.when(inside(-dx, -dy))
                def _():
                    copy(dx, dy, part).wait_recv()

        widen(part, 0, margin)
        widen(part, margin + tall, margin)
        return lax.fori_loop(part * steps, (part + 1) * steps, slab, carry)

    lax.fori_loop(0, PARTS, take_ends, 0)

    def one_line(j, ky, sums):
        base = pl.multiple_of((j * half + ky) * PITCH, 8)
        right = jnp.concatenate(
            [second[t, pl.ds(base, 2 * length), :].astype(jnp.bfloat16) for t in range(pieces)],
            axis=1,
        )
        three = jnp.dot(table_z[...], right, preferred_element_type=jnp.float32)
        re1, im1 = three[:length, :lanes], three[length:, :lanes]
        re2, im2 = three[:length, lanes:], three[length:, lanes:]
        size = (re1 * re1 + im1 * im1) * (re2 * re2 + im2 * im2)
        scale = 1.0 / (jnp.sqrt(size) + 1.0)
        real_r = ((re1 * re2 + im1 * im2) * scale).astype(jnp.bfloat16)
        imag_r = ((im1 * re2 - re1 * im2) * scale).astype(jnp.bfloat16)
        both = jnp.concatenate([real_r, imag_r], axis=0)
        along = jnp.dot(table_e[j], both, preferred_element_type=jnp.float32)
        own_rows = along[:8]
        for i in range(1, grid_x):
            own_rows = jnp.where(group == i, along[8 * i : 8 * i + 8], own_rows)
        new = []
        for o in range(3):
            new.append(sums[2 * o] + own_rows * cos_y[j, o, pl.ds(ky, 1), :])
            new.append(sums[2 * o + 1] + own_rows * sin_y[j, o, pl.ds(ky, 1), :])
        return tuple(new)

    def line(step, sums):
        for i in range(LINES):
            ky = step * LINES + i
            sums = tuple(one_line(j, ky, sums[j]) for j in range(grid_y))
        return sums

    zero = jnp.zeros((8, lanes), jnp.float32)
    sums = lax.fori_loop(0, half // LINES, line, ((zero,) * 6,) * grid_y)
    for i in range(half // LINES * LINES, half):
        sums = tuple(one_line(j, i, sums[j]) for j in range(grid_y))
    measure_peaks(grid_x, grid_y, length, peaks, valid, sums, group, mine, moved)
    sweep(grid_x, grid_y, float(length // 2), mine, moved, inbox, grid, sweep_send, sweep_recv)

    def sent(part, carry):
        for dx, dy in SIDES:

            @pl.when(inside(dx, dy))
            def _():
                copy(dx, dy, part).wait_send()

        return carry

    lax.fori_loop(0, PARTS, sent, 0)


def body(volumes, peaks, valid):
    length = volumes.shape[1]
    margin = length // 4
    half = length // 2 + 1
    _, grid_y, grid_x = peaks.shape
    lanes = grid_x * length
    tall, own = volumes.shape[2:]
    height = tall + 2 * margin
    table_x, table_y, table_z = tables(length, grid_x, grid_y)
    far_x, far_y = reach_of(grid_x, grid_y)
    deep = -(-(2 * far_y + 1) * grid_y // 8) * 8
    wide = -(-(2 * far_x + 1) * grid_x // 128) * 128
    lines = -(-half // 8) * 8
    count = len(partners(grid_x, grid_y))
    vmem = pl.BlockSpec(memory_space=pltpu.VMEM)
    smem = pl.BlockSpec(memory_space=pltpu.SMEM)
    result = pl.pallas_call(
        functools.partial(spectrum_kernel, grid_x, grid_y),
        out_shape=jax.ShapeDtypeStruct((4, grid_y, grid_x), jnp.float32),
        in_specs=[vmem] * 6 + [smem] * 2,
        out_specs=vmem,
        scratch_shapes=[
            pltpu.VMEM((grid_y, grid_x * 8, 2 * length), jnp.bfloat16),
            pltpu.VMEM((grid_y, 3, lines, lanes), jnp.float32),
            pltpu.VMEM((grid_y, 3, lines, lanes), jnp.float32),
            pltpu.VMEM((2, length, height, 2 * lanes), jnp.bfloat16),
            pltpu.VMEM((2 * lanes // 128, table_y.shape[0] // 2 * PITCH, 128), jnp.float32),
            pltpu.VMEM((2, length // GROUP, 2, tall, GROUP * margin), jnp.bfloat16),
            pltpu.VMEM((2, 2, length, margin, own), jnp.bfloat16),
            pltpu.VMEM((2, length // GROUP, 2, height, GROUP * margin), jnp.bfloat16),
            pltpu.VMEM((2, length, height, own), jnp.bfloat16),
            pltpu.SemaphoreType.DMA((len(SIDES), PARTS)),
            pltpu.SemaphoreType.DMA((len(SIDES), PARTS)),
            pltpu.VMEM((4 * grid_y, wide), jnp.float32),
            pltpu.VMEM((count, 4 * grid_y, wide), jnp.float32),
            pltpu.VMEM((4, deep, wide), jnp.float32),
            pltpu.SemaphoreType.DMA((count,)),
            pltpu.SemaphoreType.DMA((count,)),
        ],
        compiler_params=pltpu.CompilerParams(
            vmem_limit_bytes=60 * 1024 * 1024, collective_id=0, has_side_effects=True
        ),
        name="correlate",
    )(volumes, *strip_tables(margin, own), table_x, table_y, table_z, peaks, valid)
    return (result[:3], result[3])


def solution(mesh):
    return jax.shard_map(
        body,
        mesh=mesh,
        in_specs=(P(None, None, "gy", "gx"), P(None, "gy", "gx"), P("gy", "gx")),
        out_specs=(P(None, "gy", "gx"), P("gy", "gx")),
        check_vma=False,
    )
```
